512 devices in a mesh: rep: 32 (over y, x), tp: 16 (over z, core).
Axes of the slice: x: 4, y: 8, z: 8, core: 2. Of those that a mesh axis runs over, the one named last changes fastest.
Arguments:
- activations: bfloat16 [65536, 4096], P('rep', 'tp'), may hold values from -40 to 40
- out_grad: bfloat16 [65536, 1024], P(('rep', 'tp')), may hold values from -0.110485435 to 0.110485435
- weight: bfloat16 [4096, 1024], P(('tp', 'rep')), may hold values from -0.09375 to 0.09375
- momentum: float32 [4096, 1024], P(('tp', 'rep')), may hold values from -3 to 3
Outputs:
- new_weight: bfloat16 [4096, 1024], P(('tp', 'rep'))
- new_momentum: float32 [4096, 1024], P(('tp', 'rep'))
The draws below stay inside these ranges and needn't reach their ends.
All inputs are finite; a program needn't handle non-finite values.
Results may differ from the reference program's by a relative error of at most 0.0012.
Values may be sent and summed in bfloat16 or wider, within the bound.
A program may use at most 64 MiB of HBM per device.

```python
import math
import jax
import jax.numpy as jnp
from jax import lax

D = 4096
TOK = 2048
KVW = 1024
LEVELS = 5
N_REP = 32
N_TP = 16


def mixture(key, rows, cols, shared_weight):
    key_shared = jax.random.fold_in(key, 11)
    key_single = jax.random.fold_in(key, 12)
    shared = jax.random.normal(key_shared, (rows, cols), jnp.float32)
    single = jax.random.normal(key_single, (rows * N_REP, cols), jnp.float32)
    other = jnp.sqrt(1.0 - shared_weight * shared_weight)
    return shared_weight * jnp.tile(shared, (N_REP, 1)) + other * single


def column_profile(key, base):
    shard_cols = D // N_TP
    index = jnp.arange(D)
    position_all = index.astype(jnp.float32) / D
    position_local = (index % shard_cols).astype(jnp.float32) / shard_cols
    rough = jnp.exp(jax.random.uniform(jax.random.fold_in(key, 5), (D,), jnp.float32, 0.0, math.log(2.0)))
    column_scale = 0.3 * rough * jnp.exp(math.log(base) * (position_all + position_local))
    jitter = jax.random.uniform(jax.random.fold_in(key, 6), (D,), jnp.float32, -0.1, 0.1)
    shared_weight = jnp.clip(0.9 - 0.6 * position_local - 0.2 * position_all + jitter, 0.02, 0.98)
    return (column_scale, shared_weight)


def replica_scale(key):
    replica = jnp.arange(N_REP)
    log_scale = jnp.zeros((N_REP,), jnp.float32)
    for level in range(LEVELS):
        groups = N_REP // 2 ** level
        terms = jax.random.uniform(jax.random.fold_in(key, 20 + level), (groups,), jnp.float32, -1.0, 1.0)
        log_scale = log_scale + 0.45 * terms[replica // 2 ** level]
    log_scale = jnp.clip(log_scale, -1.3, 1.3)
    return jnp.repeat(jnp.exp(log_scale), TOK)


def draw_activations(key, part):
    key = jax.random.fold_in(key, 3)
    column_scale, shared_weight = column_profile(key, 3.0)
    values = mixture(key, TOK, D, shared_weight[None, :])
    values = jnp.clip(values * column_scale[None, :], -40.0, 40.0)
    return values.astype(jnp.bfloat16)


def draw_out_grad(key, part):
    key = jax.random.fold_in(key, 7)
    values = mixture(key, TOK, KVW, 0.8)
    row_scale = replica_scale(key)
    limit = 5.0 * TOK ** (-0.5)
    values = jnp.clip(values * row_scale[:, None] * (0.3 * TOK ** (-0.5)), -limit, limit)
    return values.astype(jnp.bfloat16)


def shard_levels(own_key, shape, cuts, smallest, top_value):
    def one(dim, parts):
        draws = jax.random.uniform(jax.random.fold_in(jax.random.fold_in(own_key, 6), dim), (parts,), jnp.float32, smallest / len(cuts), top_value / len(cuts))
        return jnp.repeat(jnp.exp(draws), shape[dim] // parts).reshape((-1,) + (1,) * (len(shape) - dim - 1))

    loudness = one(*cuts[0])
    for cut in cuts[1:]:
        loudness = loudness * one(*cut)
    return loudness


def gaussian(own_key, shape, deviation, bound, pieces=(), held_as=jnp.bfloat16):
    drawn = jax.random.normal(own_key, shape, jnp.float32) * deviation
    if len(pieces) > 0:
        drawn = shard_levels(own_key, shape, pieces, -0.22, 0.18) * drawn
    return jnp.clip(drawn, min=-bound, max=bound).astype(held_as)


def setup_inputs(seed: int = 0) -> dict:
    keys = jax.random.split(jax.random.key(seed), 5)
    return {
        "activations": draw_activations(jax.random.fold_in(keys[4], 71), 0),
        "out_grad": draw_out_grad(jax.random.fold_in(keys[4], 71), 0),
        "weight": gaussian(keys[2], (D, KVW), D ** -0.5, 0.09375, ((0, 512),)),
        "momentum": gaussian(keys[3], (D, KVW), 0.5, 3.0, ((0, 512),), jnp.float32),
    }


momentum_decay = 0.9
learning_rate = 0.02


def per_replica(paired):
    return lax.dot_general(paired[0], paired[1], (((0,), (0,)), ((), ())), preferred_element_type=jnp.float32)


def reference(activations, out_grad, weight, momentum):
    features = activations.reshape(N_REP, TOK, D)
    cotangent = out_grad.reshape(N_REP, TOK, KVW)
    gradients = lax.map(per_replica, (features, cotangent))
    for level in range(LEVELS):
        paired = gradients.reshape(-1, 2, D, KVW)
        lower_part = paired[:, 0]
        upper_part = paired[:, 1]
        inner = jnp.sum(lower_part * upper_part, axis=(1, 2))
        norm_lower = jnp.sum(lower_part * lower_part, axis=(1, 2))
        norm_upper = jnp.sum(upper_part * upper_part, axis=(1, 2))
        factor_lower = (1.0 - inner / (2.0 * norm_lower))[:, None, None]
        factor_upper = (1.0 - inner / (2.0 * norm_upper))[:, None, None]
        gradients = factor_lower * lower_part + factor_upper * upper_part
    combined = gradients[0]
    new_momentum = momentum_decay * momentum + combined
    new_weight = (weight.astype(jnp.float32) - learning_rate * new_momentum).astype(jnp.bfloat16)
    return new_weight, new_momentum
```

```python
import functools

import jax
import jax.numpy as jnp
from jax import lax
from jax.experimental import pallas as pl
from jax.experimental.pallas import tpu as pltpu
from jax.sharding import PartitionSpec as P

MOMENTUM_DECAY = 0.9
LEARNING_RATE = 0.02

NX, NY, NZ = 4, 8, 8
N_REP = NX * NY
N_TP = 2 * NZ
TOKENS = 2048
BLOCK = TOKENS // N_TP
FEATURES = 256
COLUMNS = 1024
ROWS = FEATURES // N_REP
CHUNKS = 8
WIDTH = COLUMNS // CHUNKS
HALF = BLOCK // 2
LANES = 128
FOLD = LANES // N_REP

MESH = pl.DeviceIdType.MESH


def coefficients(gram):
    row = lax.broadcasted_iota(jnp.int32, (N_REP, LANES), 0)
    lane = lax.broadcasted_iota(jnp.int32, (N_REP, LANES), 1)
    column = lane % N_REP
    spread = jnp.broadcast_to(gram[:, None, :], (N_REP // FOLD, FOLD, LANES)).reshape(N_REP, LANES)
    kept = jnp.where(lane // N_REP == row % FOLD, spread, 0.0)
    kept = kept + pltpu.roll(kept, N_REP, 1)
    block = kept + pltpu.roll(kept, 2 * N_REP, 1)
    diagonal = row == column
    weights = jnp.ones((N_REP, LANES), jnp.float32)
    for level in range(N_REP.bit_length() - 1):
        apart = 1 << level
        norm = jnp.sum(jnp.where(diagonal, block, 0.0), axis=0, keepdims=True)
        inner = jnp.sum(jnp.where(row == (column ^ apart), block, 0.0), axis=0, keepdims=True)
        across = jnp.broadcast_to(1.0 - inner / (2.0 * norm), (N_REP, LANES))
        down = jnp.sum(jnp.where(row == lane, across, 0.0), axis=1, keepdims=True)
        down = jnp.broadcast_to(down, (N_REP, LANES))
        weights = weights * down
        block = block * across * down
        upper = (column & apart) != 0
        block = block + jnp.where(
            upper, pltpu.roll(block, apart, 1), pltpu.roll(block, LANES - apart, 1)
        )
        upper = (row & apart) != 0
        block = block + jnp.where(
            upper, pltpu.roll(block, apart, 0), pltpu.roll(block, N_REP - apart, 0)
        )
    return weights


def kernel(
    a_ref, g_ref, w_ref, m_ref, new_w_ref, new_m_ref,
    a_vmem, a_t, gathered, grad, arrived, gram_own, gram_rep, gram_tp, weights, w_vmem, m_vmem,
    load_sem, own_sem, ring_send, ring_recv, pair_send, pair_recv, swap_send, swap_recv,
    gram_send, gram_recv,
):
    rep = lax.axis_index("rep")
    tp = lax.axis_index("tp")
    y, x = rep // NX, lax.rem(rep, NX)
    z, core = tp // 2, lax.rem(tp, 2)
    sibling = z * 2 + (1 - core)
    ahead = lax.rem(z + 1, NZ) * 2 + core
    behind = lax.rem(z + NZ - 1, NZ) * 2 + core

    def remote(src, dst, send_sem, recv_sem, to_rep, to_tp):
        return pltpu.make_async_remote_copy(
            src_ref=src, dst_ref=dst, send_sem=send_sem, recv_sem=recv_sem,
            device_id=(to_rep, to_tp), device_id_type=MESH,
        )

    def rep_peer(step):
        return lax.rem(y + step // NX, NY) * NX + lax.rem(x + lax.rem(step, NX), NX)

    def tp_peer(step):
        return lax.rem(tp + step, N_TP)

    loads = [
        pltpu.make_async_copy(a_ref, a_vmem, load_sem.at[0]),
        pltpu.make_async_copy(w_ref, w_vmem, load_sem.at[1]),
        pltpu.make_async_copy(m_ref, m_vmem, load_sem.at[2]),
    ]
    for copy in loads:
        copy.start()
    own_rows = pl.ds(pl.multiple_of(tp * BLOCK, BLOCK), BLOCK)
    own_copies = [
        pltpu.make_async_copy(
            g_ref.at[:, pl.ds(k * WIDTH, WIDTH)], gathered.at[k, own_rows], own_sem.at[k]
        )
        for k in range(CHUNKS)
    ]
    for copy in own_copies:
        copy.start()

    barrier = pltpu.get_barrier_semaphore()

    @pl.loop(1, N_REP)
    def _(step):
        pl.semaphore_signal(
            barrier, inc=1, device_id=(rep_peer(step), tp), device_id_type=MESH
        )

    @pl.loop(1, N_TP)
    def _(step):
        pl.semaphore_signal(
            barrier, inc=1, device_id=(rep, tp_peer(step)), device_id_type=MESH
        )

    pl.semaphore_wait(barrier, N_REP - 1 + N_TP - 1)

    def rows_from(distance, start=0, size=BLOCK):
        source = lax.rem(z + NZ + distance, NZ) * 2 + core
        return pl.ds(pl.multiple_of(source * BLOCK + start, size), size)

    def ring_step(k, stage):
        for way, to, sign in ((0, ahead, -1), (1, behind, 1)):
            if stage == 0:
                rows = own_rows
                src = g_ref.at[:, pl.ds(k * WIDTH, WIDTH)]
            else:
                if stage < NZ // 2:
                    rows = rows_from(sign * stage)
                else:
                    rows = rows_from(sign * stage, way * HALF, HALF)
                src = gathered.at[k, rows]
                remote(
                    src, src, ring_send.at[k], ring_recv.at[k, way, stage - 1], rep, to
                ).wait_recv()
            if stage < NZ // 2:
                sent_rows, sent = rows, src
                if stage == NZ // 2 - 1:
                    sent_rows = rows_from(sign * stage, way * HALF, HALF)
                    sent = gathered.at[k, sent_rows]
                remote(
                    sent, gathered.at[k, sent_rows], ring_send.at[k],
                    ring_recv.at[k, way, stage], rep, to,
                ).start()
            if stage > 0 or way == 0:
                remote(
                    src, gathered.at[k, rows], pair_send.at[k], pair_recv.at[k], rep, sibling
                ).start()

    def swap_chunk(k):
        own_copies[k].wait()
        half_chunk = gathered.at[k, pl.ds(0, TOKENS // 2)]
        pltpu.make_async_copy(half_chunk, half_chunk, pair_recv.at[k]).wait()
        product = jnp.dot(a_t[...], gathered[k], preferred_element_type=jnp.float32)
        grad[k] = product.reshape(N_REP, ROWS, WIDTH)

        @pl.loop(1, N_REP)
        def _(step):
            peer = rep_peer(step)
            remote(
                grad.at[k, peer], arrived.at[k, rep], swap_send.at[k], swap_recv.at[k], peer, tp
            ).start()

        arrived[k, rep] = grad[k, rep]

    def gram_chunk(k):
        others = arrived.at[k, pl.ds(0, N_REP - 1)]
        pltpu.make_async_copy(others, others, swap_recv.at[k]).wait()
        total = jnp.zeros((N_REP, LANES), jnp.float32)
        for i in range(ROWS):
            part = arrived[k, :, i, :]
            high = part.astype(jnp.bfloat16)
            low = (part - high.astype(jnp.float32)).astype(jnp.bfloat16)
            high_all = jnp.concatenate([high] * FOLD, axis=0)
            low_all = jnp.concatenate([low] * FOLD, axis=0)
            for left, right in ((high, high_all), (high, low_all), (low, high_all)):
                total += lax.dot_general(
                    left, right, (((1,), (1,)), ((), ())), preferred_element_type=jnp.float32
                )
        return total

    for k in range(0, CHUNKS):
        pass

    gram = jnp.zeros((N_REP, LANES), jnp.float32)
    rounds = CHUNKS + NZ // 2 + 1
    for j in range(rounds):
        if j == 1:
            loads[0].wait()
            for i in range(TOKENS // FEATURES):
                span = pl.ds(i * FEATURES, FEATURES)
                a_t[:, span] = a_vmem[span, :].T
        for stage in range(NZ // 2, -1, -1):
            k = j - stage
            if 0 <= k < CHUNKS:
                ring_step(k, stage)
        k = j - NZ // 2
        if 0 <= k < CHUNKS:
            swap_chunk(k)
        if 0 <= k - 1 < CHUNKS:
            gram += gram_chunk(k - 1)

    row = lax.broadcasted_iota(jnp.int32, (N_REP, LANES), 0)
    lane = lax.broadcasted_iota(jnp.int32, (N_REP, LANES), 1)
    folded = jnp.where(lane // N_REP == row % FOLD, gram, 0.0)
    folded = jnp.sum(folded.reshape(N_REP // FOLD, FOLD, LANES), axis=1)

    gram_own[0] = folded

    @pl.loop(1, N_TP)
    def _(step):
        remote(
            gram_own.at[0], gram_tp.at[tp], gram_send.at[0], gram_recv.at[0], rep, tp_peer(step)
        ).start()

    gram_tp[tp] = folded
    others = gram_tp.at[pl.ds(0, N_TP - 1)]
    pltpu.make_async_copy(others, others, gram_recv.at[0]).wait()
    replica_sum = jnp.sum(gram_tp[...], axis=0)
    gram_own[1] = replica_sum

    @pl.loop(1, N_REP)
    def _(step):
        remote(
            gram_own.at[1], gram_rep.at[rep], gram_send.at[1], gram_recv.at[1], rep_peer(step), tp
        ).start()

    gram_rep[rep] = replica_sum
    others = gram_rep.at[pl.ds(0, N_REP - 1)]
    pltpu.make_async_copy(others, others, gram_recv.at[1]).wait()
    weights[...] = coefficients(jnp.sum(gram_rep[...], axis=0))

    loads[1].wait()
    loads[2].wait()
    for k in range(CHUNKS):
        span = pl.ds(k * WIDTH, WIDTH)
        combined = jnp.zeros((ROWS, WIDTH), jnp.float32)
        for r in range(N_REP):
            combined += weights[pl.ds(r, 1), pl.ds(0, WIDTH)] * arrived[k, r]
        new_m = MOMENTUM_DECAY * m_vmem[:, span] + combined
        new_m_ref[:, span] = new_m
        new_w = w_vmem[:, span].astype(jnp.float32) - LEARNING_RATE * new_m
        new_w_ref[:, span] = new_w.astype(jnp.bfloat16)

    for k in range(CHUNKS):
        sent = gathered.at[k, pl.ds(0, 7 * BLOCK)]
        pltpu.make_async_copy(sent, sent, ring_send.at[k]).wait()
        sent = gathered.at[k, pl.ds(0, 8 * BLOCK)]
        pltpu.make_async_copy(sent, sent, pair_send.at[k]).wait()
        sent = grad.at[k, pl.ds(0, N_REP - 1)]
        pltpu.make_async_copy(sent, sent, swap_send.at[k]).wait()
    sent = gram_tp.at[pl.ds(0, N_TP - 1)]
    pltpu.make_async_copy(sent, sent, gram_send.at[0]).wait()
    sent = gram_rep.at[pl.ds(0, N_REP - 1)]
    pltpu.make_async_copy(sent, sent, gram_send.at[1]).wait()


def body(activations, out_grad, weight, momentum):
    dma = pltpu.SemaphoreType.DMA
    return pl.pallas_call(
        kernel,
        out_shape=(
            jax.ShapeDtypeStruct(weight.shape, jnp.bfloat16),
            jax.ShapeDtypeStruct(momentum.shape, jnp.float32),
        ),
        in_specs=[pl.BlockSpec(memory_space=pl.ANY)] * 4,
        out_specs=(pl.BlockSpec(memory_space=pltpu.VMEM),) * 2,
        scratch_shapes=[
            pltpu.VMEM((TOKENS, FEATURES), jnp.bfloat16),
            pltpu.VMEM((FEATURES, TOKENS), jnp.bfloat16),
            pltpu.VMEM((CHUNKS, TOKENS, WIDTH), jnp.bfloat16),
            pltpu.VMEM((CHUNKS, N_REP, ROWS, WIDTH), jnp.float32),
            pltpu.VMEM((CHUNKS, N_REP, ROWS, WIDTH), jnp.float32),
            pltpu.VMEM((2, ROWS, LANES), jnp.float32),
            pltpu.VMEM((N_REP, ROWS, LANES), jnp.float32),
            pltpu.VMEM((N_TP, ROWS, LANES), jnp.float32),
            pltpu.VMEM((N_REP, LANES), jnp.float32),
            pltpu.VMEM((ROWS, COLUMNS), jnp.bfloat16),
            pltpu.VMEM((ROWS, COLUMNS), jnp.float32),
            dma((3,)),
            dma((CHUNKS,)),
            dma((CHUNKS,)),
            dma((CHUNKS, 2, NZ // 2)),
            dma((CHUNKS,)),
            dma((CHUNKS,)),
            dma((CHUNKS,)),
            dma((CHUNKS,)),
            dma((2,)),
            dma((2,)),
        ],
        compiler_params=pltpu.CompilerParams(
            collective_id=0, has_side_effects=True, vmem_limit_bytes=48 * 1024 * 1024
        ),
    )(activations, out_grad, weight, momentum)


def solution(mesh):
    return jax.shard_map(
        body,
        mesh=mesh,
        in_specs=(
            P("rep", "tp"),
            P(("rep", "tp"), None),
            P(("tp", "rep"), None),
            P(("tp", "rep"), None),
        ),
        out_specs=(P(("tp", "rep"), None), P(("tp", "rep"), None)),
        check_vma=False,
    )
```

```python
import functools

import jax
import jax.numpy as jnp
from jax import lax
from jax.experimental import pallas as pl
from jax.experimental.pallas import tpu as pltpu
from jax.sharding import PartitionSpec as P

MOMENTUM_DECAY = 0.9
LEARNING_RATE = 0.02

NX, NY, NZ = 4, 8, 8
N_REP = NX * NY
N_TP = 2 * NZ
TOKENS = 2048
BLOCK = TOKENS // N_TP
FEATURES = 256
COLUMNS = 1024
ROWS = FEATURES // N_REP
CHUNKS = 4
WIDTH = COLUMNS // CHUNKS
HALF = BLOCK // 2
LANES = 128
FOLD = LANES // N_REP
PARTS = WIDTH // LANES
PACKED = ROWS * PARTS
GAP = 3
LOW_AFTER = 2

MESH = pl.DeviceIdType.MESH


def ring_order():
    sent, order, slot = [[] for _ in range(CHUNKS)], [], 0.0
    while len(order) < CHUNKS * (NZ // 2 + 1):
        for k in range(CHUNKS):
            stage = len(sent[k])
            if stage <= NZ // 2 and (stage == 0 or sent[k][-1] + GAP <= slot):
                sent[k].append(slot)
                order.append((k, stage))
                if stage < NZ // 2:
                    slot += 0.5 if stage == NZ // 2 - 1 else 1.0
                break
        else:
            slot += 0.5
    return order


def coefficients(gram):
    row = lax.broadcasted_iota(jnp.int32, (N_REP, LANES), 0)
    lane = lax.broadcasted_iota(jnp.int32, (N_REP, LANES), 1)
    column = lane % N_REP
    spread = jnp.broadcast_to(gram[:, None, :], (N_REP // FOLD, FOLD, LANES)).reshape(N_REP, LANES)
    kept = jnp.where(lane // N_REP == row % FOLD, spread, 0.0)
    kept = kept + pltpu.roll(kept, N_REP, 1)
    block = kept + pltpu.roll(kept, 2 * N_REP, 1)
    diagonal = row == column
    weights = jnp.ones((N_REP, LANES), jnp.float32)
    for level in range(N_REP.bit_length() - 1):
        apart = 1 << level
        norm = jnp.sum(jnp.where(diagonal, block, 0.0), axis=0, keepdims=True)
        inner = jnp.sum(jnp.where(row == (column ^ apart), block, 0.0), axis=0, keepdims=True)
        across = jnp.broadcast_to(1.0 - inner / (2.0 * norm), (N_REP, LANES))
        down = jnp.sum(jnp.where(row == lane, across, 0.0), axis=1, keepdims=True)
        down = jnp.broadcast_to(down, (N_REP, LANES))
        weights = weights * down
        block = block * across * down
        upper = (column & apart) != 0
        block = block + jnp.where(
            upper, pltpu.roll(block, apart, 1), pltpu.roll(block, LANES - apart, 1)
        )
        upper = (row & apart) != 0
        block = block + jnp.where(
            upper, pltpu.roll(block, apart, 0), pltpu.roll(block, N_REP - apart, 0)
        )
    return weights


def kernel(
    a_ref, g_ref, w_ref, m_ref, new_w_ref, new_m_ref,
    a_vmem, a_t, gathered, high_own, low_own, high_in, low_in, full,
    gram_own, gram_rep, gram_tp, weights, w_vmem, m_vmem,
    load_sem, own_sem, ring_send, ring_recv, pair_send, pair_recv, high_send, high_recv,
    low_send, low_recv, gram_send, gram_recv,
):
    rep = lax.axis_index("rep")
    tp = lax.axis_index("tp")
    y, x = rep // NX, lax.rem(rep, NX)
    z, core = tp // 2, lax.rem(tp, 2)
    sibling = z * 2 + (1 - core)
    ahead = lax.rem(z + 1, NZ) * 2 + core
    behind = lax.rem(z + NZ - 1, NZ) * 2 + core
    in_x = [lax.rem(x + d, NX) for d in range(NX)]
    far_x = sorted(range(NX), key=lambda d: -min(d, NX - d))
    far_y = sorted(range(NY), key=lambda d: -min(d, NY - d))
    far_z = sorted(range(NZ), key=lambda d: -min(d, NZ - d))
    in_y = [lax.rem(y + d, NY) * NX for d in range(NY)]
    rep_peers = [in_y[dy] + in_x[dx] for dy in far_y for dx in far_x if dy or dx]
    in_z = [lax.rem(z + d, NZ) * 2 for d in range(NZ)]
    tp_peers = [in_z[dz] + (core if same else 1 - core) for dz in far_z for same in (0, 1) if dz or not same]

    def remote(src, dst, send_sem, recv_sem, to_rep, to_tp):
        return pltpu.make_async_remote_copy(
            src_ref=src, dst_ref=dst, send_sem=send_sem, recv_sem=recv_sem,
            device_id=(to_rep, to_tp), device_id_type=MESH,
        )

    def wait_bytes(ref, sem):
        pltpu.make_async_copy(ref, ref, sem).wait()

    loads = [
        pltpu.make_async_copy(a_ref, a_vmem, load_sem.at[0]),
        pltpu.make_async_copy(w_ref, w_vmem, load_sem.at[1]),
        pltpu.make_async_copy(m_ref, m_vmem, load_sem.at[2]),
    ]
    own_rows = pl.ds(pl.multiple_of(tp * BLOCK, BLOCK), BLOCK)
    own_copies = [
        pltpu.make_async_copy(
            g_ref.at[:, pl.ds(k * WIDTH, WIDTH)], gathered.at[k, own_rows], own_sem.at[k]
        )
        for k in range(CHUNKS)
    ]

    barrier = pltpu.get_barrier_semaphore()
    for peer in tp_peers[::-1]:
        pl.semaphore_signal(barrier, inc=1, device_id=(rep, peer), device_id_type=MESH)
    for peer in rep_peers:
        pl.semaphore_signal(barrier, inc=1, device_id=(peer, tp), device_id_type=MESH)
    for copy in loads + own_copies:
        copy.start()
    loads[0].wait()
    for i in range(TOKENS // FEATURES):
        span = pl.ds(i * FEATURES, FEATURES)
        a_t[:, span] = a_vmem[span, :].T
    pl.semaphore_wait(barrier, N_REP - 1 + N_TP - 1)

    def rows_from(distance, start=0, size=BLOCK):
        source = lax.rem(z + NZ + distance, NZ) * 2 + core
        return pl.ds(pl.multiple_of(source * BLOCK + start, size), size)

    def ring_step(k, stage):
        for way, to, sign in ((0, ahead, -1), (1, behind, 1)):
            if stage == 0:
                rows = own_rows
                src = g_ref.at[:, pl.ds(k * WIDTH, WIDTH)]
            else:
                if stage < NZ // 2:
                    rows = rows_from(sign * stage)
                else:
                    rows = rows_from(sign * stage, way * HALF, HALF)
                src = gathered.at[k, rows]
                remote(
                    src, src, ring_send.at[k], ring_recv.at[k, way, stage - 1], rep, to
                ).wait_recv()
            if stage < NZ // 2:
                sent_rows, sent = rows, src
                if stage == NZ // 2 - 1:
                    sent_rows = rows_from(sign * stage, way * HALF, HALF)
                    sent = gathered.at[k, sent_rows]
                remote(
                    sent, gathered.at[k, sent_rows], ring_send.at[k],
                    ring_recv.at[k, way, stage], rep, to,
                ).start()
            if stage > 0 or way == 0:
                remote(
                    src, gathered.at[k, rows], pair_send.at[k], pair_recv.at[k], rep, sibling
                ).start()

    def send_rows(own, into, send_sem, recv_sem, k):
        def to(peer):
            remote(
                own.at[k, peer], into.at[k, rep], send_sem.at[k], recv_sem.at[k], peer, tp
            ).start()

        def to_row(dy):
            row = lax.rem(y + dy, NY) * NX
            for dx in far_x:
                to(row + in_x[dx])

        to_row(NY // 2)

        @pl.loop(1, NY // 2)
        def _(step):
            to_row(NY // 2 - step)
            to_row(NY // 2 + step)

        for dx in far_x:
            if dx:
                to(y * NX + in_x[dx])
        into[k, rep] = own[k, rep]

    def send_high(k):
        own_copies[k].wait()
        wait_bytes(gathered.at[k, pl.ds(0, TOKENS // 2)], pair_recv.at[k])
        product = jnp.dot(a_t[...], gathered[k], preferred_element_type=jnp.float32)
        product = jnp.concatenate(
            [
                product[:, p * LANES:(p + 1) * LANES].reshape(N_REP, ROWS, LANES)
                for p in range(PARTS)
            ],
            axis=1,
        )
        high = product.astype(jnp.bfloat16)
        high_own[k] = high
        send_rows(high_own, high_in, high_send, high_recv, k)
        low_own[k] = (product - high.astype(jnp.float32)).astype(jnp.bfloat16)

    def send_low(k):
        send_rows(low_own, low_in, low_send, low_recv, k)

    def gram_chunk(k):
        wait_bytes(high_in.at[k, pl.ds(0, N_REP - 1)], high_recv.at[k])
        full[k] = high_in[k].astype(jnp.float32)
        total = jnp.zeros((N_REP, LANES), jnp.float32)
        for i in range(0, PACKED, 2):
            part = jnp.concatenate([full[k, :, i, :], full[k, :, i + 1, :]], axis=1)
            part = part.astype(jnp.bfloat16)
            total += lax.dot_general(
                part, jnp.concatenate([part] * FOLD, axis=0),
                (((1,), (1,)), ((), ())), preferred_element_type=jnp.float32,
            )
        return total

    done = 0
    for k, stage in ring_order():
        ring_step(k, stage)
        if stage == NZ // 2:
            send_high(k)
            done += 1
            if done < CHUNKS and done - LOW_AFTER >= 0:
                send_low(done - LOW_AFTER)
    lows = [k for k in range(CHUNKS) if not (LOW_AFTER <= k + LOW_AFTER < CHUNKS)]
    for k in lows:
        send_low(k)

    gram = jnp.zeros((N_REP, LANES), jnp.float32)
    for k in range(CHUNKS):
        gram += gram_chunk(k)

    row = lax.broadcasted_iota(jnp.int32, (N_REP, LANES), 0)
    lane = lax.broadcasted_iota(jnp.int32, (N_REP, LANES), 1)
    folded = jnp.where(lane // N_REP == row % FOLD, gram, 0.0)
    folded = jnp.sum(folded.reshape(N_REP // FOLD, FOLD, LANES), axis=1)

    gram_own[0] = folded
    for peer in tp_peers:
        remote(
            gram_own.at[0], gram_tp.at[tp], gram_send.at[0], gram_recv.at[0], rep, peer
        ).start()
    gram_tp[tp] = folded
    wait_bytes(gram_tp.at[pl.ds(0, N_TP - 1)], gram_recv.at[0])
    replica_sum = jnp.sum(gram_tp[...], axis=0)
    gram_own[1] = replica_sum
    for peer in rep_peers:
        remote(
            gram_own.at[1], gram_rep.at[rep], gram_send.at[1], gram_recv.at[1], peer, tp
        ).start()
    gram_rep[rep] = replica_sum

    for k in range(CHUNKS):
        wait_bytes(low_in.at[k, pl.ds(0, N_REP - 1)], low_recv.at[k])
        full[k] += low_in[k].astype(jnp.float32)
    loads[1].wait()
    loads[2].wait()
    for k in range(CHUNKS):
        wait_bytes(gathered.at[k, pl.ds(0, 7 * BLOCK)], ring_send.at[k])
        wait_bytes(gathered.at[k, pl.ds(0, 8 * BLOCK)], pair_send.at[k])
        wait_bytes(high_own.at[k, pl.ds(0, N_REP - 1)], high_send.at[k])
        wait_bytes(low_own.at[k, pl.ds(0, N_REP - 1)], low_send.at[k])
    wait_bytes(gram_tp.at[pl.ds(0, N_TP - 1)], gram_send.at[0])

    wait_bytes(gram_rep.at[pl.ds(0, N_REP - 1)], gram_recv.at[1])
    weights[...] = coefficients(jnp.sum(gram_rep[...], axis=0))
    for k in range(CHUNKS):
        combined = jnp.zeros((PACKED, LANES), jnp.float32)
        for r in range(N_REP):
            combined += weights[pl.ds(r, 1), :] * full[k, r]
        for p in range(PARTS):
            span = pl.ds(k * WIDTH + p * LANES, LANES)
            new_m = MOMENTUM_DECAY * m_vmem[:, span] + combined[p * ROWS:(p + 1) * ROWS]
            new_m_ref[:, span] = new_m
            new_w = w_vmem[:, span].astype(jnp.float32) - LEARNING_RATE * new_m
            new_w_ref[:, span] = new_w.astype(jnp.bfloat16)
    wait_bytes(gram_rep.at[pl.ds(0, N_REP - 1)], gram_send.at[1])


def body(activations, out_grad, weight, momentum):
    dma = pltpu.SemaphoreType.DMA
    return pl.pallas_call(
        kernel,
        out_shape=(
            jax.ShapeDtypeStruct(weight.shape, jnp.bfloat16),
            jax.ShapeDtypeStruct(momentum.shape, jnp.float32),
        ),
        in_specs=[pl.BlockSpec(memory_space=pltpu.HBM)] * 4,
        out_specs=(pl.BlockSpec(memory_space=pltpu.VMEM),) * 2,
        scratch_shapes=[
            pltpu.VMEM((TOKENS, FEATURES), jnp.bfloat16),
            pltpu.VMEM((FEATURES, TOKENS), jnp.bfloat16),
            pltpu.VMEM((CHUNKS, TOKENS, WIDTH), jnp.bfloat16),
            pltpu.VMEM((CHUNKS, N_REP, PACKED, LANES), jnp.bfloat16),
            pltpu.VMEM((CHUNKS, N_REP, PACKED, LANES), jnp.bfloat16),
            pltpu.VMEM((CHUNKS, N_REP, PACKED, LANES), jnp.bfloat16),
            pltpu.VMEM((CHUNKS, N_REP, PACKED, LANES), jnp.bfloat16),
            pltpu.VMEM((CHUNKS, N_REP, PACKED, LANES), jnp.float32),
            pltpu.VMEM((2, ROWS, LANES), jnp.float32),
            pltpu.VMEM((N_REP, ROWS, LANES), jnp.float32),
            pltpu.VMEM((N_TP, ROWS, LANES), jnp.float32),
            pltpu.VMEM((N_REP, LANES), jnp.float32),
            pltpu.VMEM((ROWS, COLUMNS), jnp.bfloat16),
            pltpu.VMEM((ROWS, COLUMNS), jnp.float32),
            dma((3,)),
            dma((CHUNKS,)),
            dma((CHUNKS,)),
            dma((CHUNKS, 2, NZ // 2)),
            dma((CHUNKS,)),
            dma((CHUNKS,)),
            dma((CHUNKS,)),
            dma((CHUNKS,)),
            dma((CHUNKS,)),
            dma((CHUNKS,)),
            dma((2,)),
            dma((2,)),
        ],
        compiler_params=pltpu.CompilerParams(
            collective_id=0, has_side_effects=True, vmem_limit_bytes=62 * 1024 * 1024
        ),
    )(activations, out_grad, weight, momentum)


def solution(mesh):
    return jax.shard_map(
        body,
        mesh=mesh,
        in_specs=(
            P("rep", "tp"),
            P(("rep", "tp"), None),
            P(("tp", "rep"), None),
            P(("tp", "rep"), None),
        ),
        out_specs=(P(("tp", "rep"), None), P(("tp", "rep"), None)),
        check_vma=False,
    )
```

```python
import functools

import jax
import jax.numpy as jnp
from jax import lax
from jax.experimental import pallas as pl
from jax.experimental.pallas import tpu as pltpu
from jax.sharding import PartitionSpec as P

MOMENTUM_DECAY = 0.9
LEARNING_RATE = 0.02

NX, NY, NZ = 4, 8, 8
N_REP = NX * NY
N_TP = 2 * NZ
TOKENS = 2048
BLOCK = TOKENS // N_TP
FEATURES = 256
COLUMNS = 1024
ROWS = FEATURES // N_REP
CHUNKS = 4
WIDTH = COLUMNS // CHUNKS
HALF = BLOCK // 2
LANES = 128
FOLD = LANES // N_REP
PARTS = WIDTH // LANES
PACKED = ROWS * PARTS

MESH = pl.DeviceIdType.MESH


ORDER = (
    (0, 0), (1, 0), (2, 0), (0, 1), (3, 0), (1, 1), (0, 2), (2, 1), (1, 2), (0, 3),
    (3, 1), (2, 2), (1, 3), (0, 4), (3, 2), (2, 3), (1, 4), (3, 3), (2, 4), (3, 4),
)
EARLY_LOW = {0: 0}
MID_LOW = (1, 2, 3)
LATE_LOW = ()
GREET = {4: 0, 7: 1, 10: 2, 12: 3}


def coefficients(gram):
    row = lax.broadcasted_iota(jnp.int32, (N_REP, LANES), 0)
    lane = lax.broadcasted_iota(jnp.int32, (N_REP, LANES), 1)
    column = lane % N_REP
    spread = jnp.broadcast_to(gram[:, None, :], (N_REP // FOLD, FOLD, LANES)).reshape(N_REP, LANES)
    kept = jnp.where(lane // N_REP == row % FOLD, spread, 0.0)
    kept = kept + pltpu.roll(kept, N_REP, 1)
    block = kept + pltpu.roll(kept, 2 * N_REP, 1)
    diagonal = row == column
    weights = jnp.ones((N_REP, LANES), jnp.float32)
    for level in range(N_REP.bit_length() - 1):
        apart = 1 << level
        norm = jnp.sum(jnp.where(diagonal, block, 0.0), axis=0, keepdims=True)
        inner = jnp.sum(jnp.where(row == (column ^ apart), block, 0.0), axis=0, keepdims=True)
        across = jnp.broadcast_to(1.0 - inner / (2.0 * norm), (N_REP, LANES))
        down = jnp.sum(jnp.where(row == lane, across, 0.0), axis=1, keepdims=True)
        down = jnp.broadcast_to(down, (N_REP, LANES))
        weights = weights * down
        block = block * across * down
        upper = (column & apart) != 0
        block = block + jnp.where(
            upper, pltpu.roll(block, apart, 1), pltpu.roll(block, LANES - apart, 1)
        )
        upper = (row & apart) != 0
        block = block + jnp.where(
            upper, pltpu.roll(block, apart, 0), pltpu.roll(block, N_REP - apart, 0)
        )
    return weights


def kernel(
    a_ref, g_ref, w_ref, m_ref, new_w_ref, new_m_ref,
    a_vmem, a_t, gathered, high_own, low_own, high_in, low_in, full,
    gram_own, gram_rep, gram_tp, weights, w_vmem, m_vmem,
    load_sem, own_sem, ring_send, ring_recv, pair_send, pair_recv, high_send, high_recv,
    low_send, low_recv, gram_send, gram_recv, greet_sem,
):
    rep = lax.axis_index("rep")
    tp = lax.axis_index("tp")
    y, x = rep // NX, lax.rem(rep, NX)
    z, core = tp // 2, lax.rem(tp, 2)
    sibling = z * 2 + (1 - core)
    ahead = lax.rem(z + 1, NZ) * 2 + core
    behind = lax.rem(z + NZ - 1, NZ) * 2 + core
    in_x = [lax.rem(x + d, NX) for d in range(NX)]
    far_x = sorted(range(NX), key=lambda d: -min(d, NX - d))
    far_y = sorted(range(NY), key=lambda d: -min(d, NY - d))
    far_z = sorted(range(NZ), key=lambda d: -min(d, NZ - d))
    in_y = [lax.rem(y + d, NY) * NX for d in range(NY)]
    rep_peers = [in_y[dy] + in_x[dx] for dy in far_y for dx in far_x if dy or dx]
    in_z = [lax.rem(z + d, NZ) * 2 for d in range(NZ)]
    tp_peers = [in_z[dz] + (core if same else 1 - core) for dz in far_z for same in (0, 1) if dz or not same]

    def remote(src, dst, send_sem, recv_sem, to_rep, to_tp):
        return pltpu.make_async_remote_copy(
            src_ref=src, dst_ref=dst, send_sem=send_sem, recv_sem=recv_sem,
            device_id=(to_rep, to_tp), device_id_type=MESH,
        )

    def wait_bytes(ref, sem):
        pltpu.make_async_copy(ref, ref, sem).wait()

    loads = [
        pltpu.make_async_copy(a_ref, a_vmem, load_sem.at[0]),
        pltpu.make_async_copy(w_ref, w_vmem, load_sem.at[1]),
        pltpu.make_async_copy(m_ref, m_vmem, load_sem.at[2]),
    ]
    own_rows = pl.ds(pl.multiple_of(tp * BLOCK, BLOCK), BLOCK)
    own_copies = [
        pltpu.make_async_copy(
            g_ref.at[:, pl.ds(k * WIDTH, WIDTH)], gathered.at[k, own_rows], own_sem.at[k]
        )
        for k in range(CHUNKS)
    ]

    barrier = pltpu.get_barrier_semaphore()
    for peer in (sibling, ahead, behind):
        pl.semaphore_signal(barrier, inc=1, device_id=(rep, peer), device_id_type=MESH)
    for peer in [in_y[0] + in_x[d] for d in range(1, NX)] + [in_y[d] + x for d in (1, NY - 1)]:
        pl.semaphore_signal(barrier, inc=1, device_id=(peer, tp), device_id_type=MESH)

    def greet(turn):
        for d in (1, NY - 1):
            pl.semaphore_signal(
                greet_sem.at[turn], inc=1, device_id=(in_y[d] + x, tp), device_id_type=MESH
            )

    for copy in loads + own_copies:
        copy.start()
    loads[0].wait()
    for i in range(TOKENS // FEATURES):
        span = pl.ds(i * FEATURES, FEATURES)
        a_t[:, span] = a_vmem[span, :].T
    pl.semaphore_wait(barrier, 3 + NX - 1 + 2)
    greet(0)

    def rows_from(distance, start=0, size=BLOCK):
        source = lax.rem(z + NZ + distance, NZ) * 2 + core
        return pl.ds(pl.multiple_of(source * BLOCK + start, size), size)

    def ring_step(k, stage):
        for way, to, sign in ((0, ahead, -1), (1, behind, 1)):
            if stage == 0:
                rows = own_rows
                src = g_ref.at[:, pl.ds(k * WIDTH, WIDTH)]
            else:
                if stage < NZ // 2:
                    rows = rows_from(sign * stage)
                else:
                    rows = rows_from(sign * stage, way * HALF, HALF)
                src = gathered.at[k, rows]
                remote(
                    src, src, ring_send.at[k], ring_recv.at[k, way, stage - 1], rep, to
                ).wait_recv()
            if stage < NZ // 2:
                sent_rows, sent = rows, src
                if stage == NZ // 2 - 1:
                    sent_rows = rows_from(sign * stage, way * HALF, HALF)
                    sent = gathered.at[k, sent_rows]
                remote(
                    sent, gathered.at[k, sent_rows], ring_send.at[k],
                    ring_recv.at[k, way, stage], rep, to,
                ).start()
            if stage > 0 or way == 0:
                remote(
                    src, gathered.at[k, rows], pair_send.at[k], pair_recv.at[k], rep, sibling
                ).start()

    def send_rows(own, into, send_sem, recv_sem, k):
        def to(peer):
            remote(
                own.at[k, peer], into.at[k, rep], send_sem.at[k], recv_sem.at[k], peer, tp
            ).start()

        def to_row(dy):
            row = lax.rem(y + dy, NY) * NX
            for dx in far_x:
                to(row + in_x[dx])

        to_row(NY // 2)

        @pl.loop(1, NY // 2)
        def _(step):
            to_row(NY // 2 - step)
            to_row(NY // 2 + step)

        for dx in far_x:
            if dx:
                to(y * NX + in_x[dx])
        into[k, rep] = own[k, rep]

    def send_high(k):
        own_copies[k].wait()
        wait_bytes(gathered.at[k, pl.ds(0, TOKENS // 2)], pair_recv.at[k])
        product = jnp.dot(a_t[...], gathered[k], preferred_element_type=jnp.float32)
        product = jnp.concatenate(
            [
                product[:, p * LANES:(p + 1) * LANES].reshape(N_REP, ROWS, LANES)
                for p in range(PARTS)
            ],
            axis=1,
        )
        high = product.astype(jnp.bfloat16)
        high_own[k] = high
        send_rows(high_own, high_in, high_send, high_recv, k)
        low_own[k] = (product - high.astype(jnp.float32)).astype(jnp.bfloat16)

    def send_low(k):
        send_rows(low_own, low_in, low_send, low_recv, k)

    def gram_chunk(k):
        wait_bytes(high_in.at[k, pl.ds(0, N_REP - 1)], high_recv.at[k])
        full[k] = high_in[k].astype(jnp.float32)
        total = jnp.zeros((N_REP, LANES), jnp.float32)
        for i in range(0, PACKED, 2):
            part = jnp.concatenate([full[k, :, i, :], full[k, :, i + 1, :]], axis=1)
            part = part.astype(jnp.bfloat16)
            total += lax.dot_general(
                part, jnp.concatenate([part] * FOLD, axis=0),
                (((1,), (1,)), ((), ())), preferred_element_type=jnp.float32,
            )
        return total

    for i, (k, stage) in enumerate(ORDER):
        if i in GREET:
            turn = GREET[i]
            pl.semaphore_wait(greet_sem.at[turn], 2)
            if turn + 1 < NY // 2:
                greet(turn + 1)
        ring_step(k, stage)
        if stage == NZ // 2:
            send_high(k)
            if k in EARLY_LOW:
                send_low(EARLY_LOW[k])
    for k in MID_LOW:
        send_low(k)

    gram = jnp.zeros((N_REP, LANES), jnp.float32)
    for k in range(CHUNKS):
        gram += gram_chunk(k)

    row = lax.broadcasted_iota(jnp.int32, (N_REP, LANES), 0)
    lane = lax.broadcasted_iota(jnp.int32, (N_REP, LANES), 1)
    folded = jnp.where(lane // N_REP == row % FOLD, gram, 0.0)
    folded = jnp.sum(folded.reshape(N_REP // FOLD, FOLD, LANES), axis=1)

    gram_own[0] = folded
    for peer in tp_peers:
        remote(
            gram_own.at[0], gram_tp.at[tp], gram_send.at[0], gram_recv.at[0], rep, peer
        ).start()
    for k in LATE_LOW:
        send_low(k)
    gram_tp[tp] = folded
    wait_bytes(gram_tp.at[pl.ds(0, N_TP - 1)], gram_recv.at[0])
    replica_sum = jnp.sum(gram_tp[...], axis=0)
    gram_own[1] = replica_sum
    for peer in rep_peers:
        remote(
            gram_own.at[1], gram_rep.at[rep], gram_send.at[1], gram_recv.at[1], peer, tp
        ).start()
    gram_rep[rep] = replica_sum

    for k in range(CHUNKS):
        wait_bytes(low_in.at[k, pl.ds(0, N_REP - 1)], low_recv.at[k])
        full[k] += low_in[k].astype(jnp.float32)
    loads[1].wait()
    loads[2].wait()
    for k in range(CHUNKS):
        wait_bytes(gathered.at[k, pl.ds(0, 7 * BLOCK)], ring_send.at[k])
        wait_bytes(gathered.at[k, pl.ds(0, 8 * BLOCK)], pair_send.at[k])
        wait_bytes(high_own.at[k, pl.ds(0, N_REP - 1)], high_send.at[k])
        wait_bytes(low_own.at[k, pl.ds(0, N_REP - 1)], low_send.at[k])
    wait_bytes(gram_tp.at[pl.ds(0, N_TP - 1)], gram_send.at[0])

    wait_bytes(gram_rep.at[pl.ds(0, N_REP - 1)], gram_recv.at[1])
    weights[...] = coefficients(jnp.sum(gram_rep[...], axis=0))
    for k in range(CHUNKS):
        combined = jnp.zeros((PACKED, LANES), jnp.float32)
        for r in range(N_REP):
            combined += weights[pl.ds(r, 1), :] * full[k, r]
        for p in range(PARTS):
            span = pl.ds(k * WIDTH + p * LANES, LANES)
            new_m = MOMENTUM_DECAY * m_vmem[:, span] + combined[p * ROWS:(p + 1) * ROWS]
            new_m_ref[:, span] = new_m
            new_w = w_vmem[:, span].astype(jnp.float32) - LEARNING_RATE * new_m
            new_w_ref[:, span] = new_w.astype(jnp.bfloat16)
    wait_bytes(gram_rep.at[pl.ds(0, N_REP - 1)], gram_send.at[1])


def body(activations, out_grad, weight, momentum):
    dma = pltpu.SemaphoreType.DMA
    return pl.pallas_call(
        kernel,
        out_shape=(
            jax.ShapeDtypeStruct(weight.shape, jnp.bfloat16),
            jax.ShapeDtypeStruct(momentum.shape, jnp.float32),
        ),
        in_specs=[pl.BlockSpec(memory_space=pltpu.HBM)] * 4,
        out_specs=(pl.BlockSpec(memory_space=pltpu.VMEM),) * 2,
        scratch_shapes=[
            pltpu.VMEM((TOKENS, FEATURES), jnp.bfloat16),
            pltpu.VMEM((FEATURES, TOKENS), jnp.bfloat16),
            pltpu.VMEM((CHUNKS, TOKENS, WIDTH), jnp.bfloat16),
            pltpu.VMEM((CHUNKS, N_REP, PACKED, LANES), jnp.bfloat16),
            pltpu.VMEM((CHUNKS, N_REP, PACKED, LANES), jnp.bfloat16),
            pltpu.VMEM((CHUNKS, N_REP, PACKED, LANES), jnp.bfloat16),
            pltpu.VMEM((CHUNKS, N_REP, PACKED, LANES), jnp.bfloat16),
            pltpu.VMEM((CHUNKS, N_REP, PACKED, LANES), jnp.float32),
            pltpu.VMEM((2, ROWS, LANES), jnp.float32),
            pltpu.VMEM((N_REP, ROWS, LANES), jnp.float32),
            pltpu.VMEM((N_TP, ROWS, LANES), jnp.float32),
            pltpu.VMEM((N_REP, LANES), jnp.float32),
            pltpu.VMEM((ROWS, COLUMNS), jnp.bfloat16),
            pltpu.VMEM((ROWS, COLUMNS), jnp.float32),
            dma((3,)),
            dma((CHUNKS,)),
            dma((CHUNKS,)),
            dma((CHUNKS, 2, NZ // 2)),
            dma((CHUNKS,)),
            dma((CHUNKS,)),
            dma((CHUNKS,)),
            dma((CHUNKS,)),
            dma((CHUNKS,)),
            dma((CHUNKS,)),
            dma((2,)),
            dma((2,)),
            pltpu.SemaphoreType.REGULAR((NY // 2,)),
        ],
        compiler_params=pltpu.CompilerParams(
            collective_id=0, has_side_effects=True, vmem_limit_bytes=62 * 1024 * 1024
        ),
    )(activations, out_grad, weight, momentum)


def solution(mesh):
    return jax.shard_map(
        body,
        mesh=mesh,
        in_specs=(
            P("rep", "tp"),
            P(("rep", "tp"), None),
            P(("tp", "rep"), None),
            P(("tp", "rep"), None),
        ),
        out_specs=(P(("tp", "rep"), None), P(("tp", "rep"), None)),
        check_vma=False,
    )
```

```python
import functools

import jax
import jax.numpy as jnp
from jax import lax
from jax.experimental import pallas as pl
from jax.experimental.pallas import tpu as pltpu
from jax.sharding import PartitionSpec as P

MOMENTUM_DECAY = 0.9
LEARNING_RATE = 0.02

NX, NY, NZ = 4, 8, 8
N_REP = NX * NY
N_TP = 2 * NZ
TOKENS = 2048
BLOCK = TOKENS // N_TP
FEATURES = 256
COLUMNS = 1024
ROWS = FEATURES // N_REP
CHUNKS = 4
WIDTH = COLUMNS // CHUNKS
HALF = BLOCK // 2
LANES = 128
FOLD = LANES // N_REP
PARTS = WIDTH // LANES
PACKED = ROWS * PARTS

MESH = pl.DeviceIdType.MESH


ORDER = (
    (0, 0), (1, 0), (2, 0), (0, 1), (3, 0), (1, 1), (0, 2), (2, 1), (1, 2), (0, 3),
    (3, 1), (2, 2), (1, 3), (0, 4), (3, 2), (2, 3), (1, 4), (3, 3), (2, 4), (3, 4),
)
TURN_AT = 3
PAIRED = {3: ((0, 4), (5, 3)), 4: ((4, 1),)}
EARLY_LOW = {0: 0}
MID_LOW = (1, 2, 3)
LATE_LOW = ()
GREET = {4: 0, 7: 1, 10: 2, 12: 3}


def coefficients(gram):
    row = lax.broadcasted_iota(jnp.int32, (N_REP, LANES), 0)
    lane = lax.broadcasted_iota(jnp.int32, (N_REP, LANES), 1)
    column = lane % N_REP
    spread = jnp.broadcast_to(gram[:, None, :], (N_REP // FOLD, FOLD, LANES)).reshape(N_REP, LANES)
    kept = jnp.where(lane // N_REP == row % FOLD, spread, 0.0)
    kept = kept + pltpu.roll(kept, N_REP, 1)
    block = kept + pltpu.roll(kept, 2 * N_REP, 1)
    diagonal = row == column
    weights = jnp.ones((N_REP, LANES), jnp.float32)
    for level in range(N_REP.bit_length() - 1):
        apart = 1 << level
        norm = jnp.sum(jnp.where(diagonal, block, 0.0), axis=0, keepdims=True)
        inner = jnp.sum(jnp.where(row == (column ^ apart), block, 0.0), axis=0, keepdims=True)
        across = jnp.broadcast_to(1.0 - inner / (2.0 * norm), (N_REP, LANES))
        down = jnp.sum(jnp.where(row == lane, across, 0.0), axis=1, keepdims=True)
        down = jnp.broadcast_to(down, (N_REP, LANES))
        weights = weights * down
        block = block * across * down
        upper = (column & apart) != 0
        block = block + jnp.where(
            upper, pltpu.roll(block, apart, 1), pltpu.roll(block, LANES - apart, 1)
        )
        upper = (row & apart) != 0
        block = block + jnp.where(
            upper, pltpu.roll(block, apart, 0), pltpu.roll(block, N_REP - apart, 0)
        )
    return weights


def kernel(
    a_ref, g_ref, out_ref,
    a_vmem, a_t, gathered, high_own, low_own, high_in, low_in, full,
    gram_own, gram_rep, gram_tp, weights,
    load_sem, own_sem, ring_send, ring_recv, pair_send, pair_recv, high_send, high_recv,
    low_send, low_recv, gram_send, gram_recv, greet_sem,
):
    rep = lax.axis_index("rep")
    tp = lax.axis_index("tp")
    y, x = rep // NX, lax.rem(rep, NX)
    z, core = tp // 2, lax.rem(tp, 2)
    sibling = z * 2 + (1 - core)
    ahead = lax.rem(z + 1, NZ) * 2 + core
    behind = lax.rem(z + NZ - 1, NZ) * 2 + core
    in_x = [lax.rem(x + d, NX) for d in range(NX)]
    far_x = sorted(range(NX), key=lambda d: -min(d, NX - d))
    far_y = sorted(range(NY), key=lambda d: -min(d, NY - d))
    far_z = sorted(range(NZ), key=lambda d: -min(d, NZ - d))
    in_y = [lax.rem(y + d, NY) * NX for d in range(NY)]
    rep_peers = [in_y[dy] + in_x[dx] for dy in far_y for dx in far_x if dy or dx]
    in_z = [lax.rem(z + d, NZ) * 2 for d in range(NZ)]
    tp_peers = [in_z[dz] + (core if same else 1 - core) for dz in far_z for same in (0, 1) if dz or not same]

    def remote(src, dst, send_sem, recv_sem, to_rep, to_tp):
        return pltpu.make_async_remote_copy(
            src_ref=src, dst_ref=dst, send_sem=send_sem, recv_sem=recv_sem,
            device_id=(to_rep, to_tp), device_id_type=MESH,
        )

    def wait_bytes(ref, sem):
        pltpu.make_async_copy(ref, ref, sem).wait()

    load = pltpu.make_async_copy(a_ref, a_vmem, load_sem)
    own_copies = [
        pltpu.make_async_copy(
            g_ref.at[:, pl.ds(k * WIDTH, WIDTH)], gathered.at[k, 0, 0], own_sem.at[k]
        )
        for k in range(CHUNKS)
    ]

    barrier = pltpu.get_barrier_semaphore()
    for peer in (sibling, ahead, behind):
        pl.semaphore_signal(barrier, inc=1, device_id=(rep, peer), device_id_type=MESH)
    for peer in [in_y[0] + in_x[d] for d in range(1, NX)] + [in_y[d] + x for d in (1, NY - 1)]:
        pl.semaphore_signal(barrier, inc=1, device_id=(peer, tp), device_id_type=MESH)

    def greet(turn):
        for d in (1, NY - 1):
            pl.semaphore_signal(
                greet_sem.at[turn], inc=1, device_id=(in_y[d] + x, tp), device_id_type=MESH
            )

    for copy in [load] + own_copies:
        copy.start()
    pl.semaphore_wait(barrier, 3 + NX - 1 + 2)
    greet(0)

    def ring_step(k, stage):
        middle = NZ // 2
        for way, to in ((0, ahead), (1, behind)):
            half = pl.ds(way * HALF, HALF)
            held, next_held = (stage, stage + 1) if way else (-stage % NZ, (-stage - 1) % NZ)
            if stage == 0:
                src = g_ref.at[:, pl.ds(k * WIDTH, WIDTH)]
            else:
                src = gathered.at[k, 0, held]
                came = gathered.at[k, 0, held, half] if stage == middle else src
                remote(
                    came, came, ring_send.at[k], ring_recv.at[k, way, stage - 1], rep, to
                ).wait_recv()
            if stage < middle:
                dst = gathered.at[k, 0, next_held]
                if stage == middle - 1:
                    src, dst = gathered.at[k, 0, held, half], gathered.at[k, 0, next_held, half]
                remote(
                    src, dst, ring_send.at[k], ring_recv.at[k, way, stage], rep, to
                ).start()
        for first, count in PAIRED.get(stage, ()):
            if first == 0:
                own_copies[k].wait()
            slots = pl.ds(first, count)
            remote(
                gathered.at[k, 0, slots], gathered.at[k, 1, slots],
                pair_send.at[k], pair_recv.at[k], rep, sibling,
            ).start()

    def send_rows(own, into, send_sem, recv_sem, k):
        def to(peer):
            remote(
                own.at[k, peer], into.at[k, rep], send_sem.at[k], recv_sem.at[k], peer, tp
            ).start()

        def to_row(dy):
            row = lax.rem(y + dy, NY) * NX
            for dx in far_x:
                to(row + in_x[dx])

        to_row(NY // 2)

        @pl.loop(1, NY // 2)
        def _(step):
            to_row(NY // 2 - step)
            to_row(NY // 2 + step)

        for dx in far_x:
            if dx:
                to(y * NX + in_x[dx])
        into[k, rep] = own[k, rep]

    def send_high(k):
        wait_bytes(gathered.at[k, 1], pair_recv.at[k])
        product = jnp.dot(
            a_t[...], gathered[k].reshape(TOKENS, WIDTH), preferred_element_type=jnp.float32
        )
        product = jnp.concatenate(
            [
                product[:, p * LANES:(p + 1) * LANES].reshape(N_REP, ROWS, LANES)
                for p in range(PARTS)
            ],
            axis=1,
        )
        high = product.astype(jnp.bfloat16)
        high_own[k] = high
        send_rows(high_own, high_in, high_send, high_recv, k)
        low_own[k] = (product - high.astype(jnp.float32)).astype(jnp.bfloat16)

    def send_low(k):
        send_rows(low_own, low_in, low_send, low_recv, k)

    def gram_chunk(k):
        wait_bytes(high_in.at[k, pl.ds(0, N_REP - 1)], high_recv.at[k])
        full[k] = high_in[k].astype(jnp.float32)
        total = jnp.zeros((N_REP, LANES), jnp.float32)
        for i in range(0, PACKED, 2):
            part = jnp.concatenate([full[k, :, i, :], full[k, :, i + 1, :]], axis=1)
            part = part.astype(jnp.bfloat16)
            total += lax.dot_general(
                part, jnp.concatenate([part] * FOLD, axis=0),
                (((1,), (1,)), ((), ())), preferred_element_type=jnp.float32,
            )
        return total

    for i, (k, stage) in enumerate(ORDER):
        if i == TURN_AT:
            load.wait()
            for j in range(N_TP):
                source = in_z[j % NZ] + (core if j < NZ else 1 - core)
                rows = pl.ds(pl.multiple_of(source * BLOCK, BLOCK), BLOCK)
                a_t[:, pl.ds(j * BLOCK, BLOCK)] = a_vmem[rows, :].T
        if i in GREET:
            turn = GREET[i]
            pl.semaphore_wait(greet_sem.at[turn], 2)
            if turn + 1 < NY // 2:
                greet(turn + 1)
        ring_step(k, stage)
        if stage == NZ // 2:
            send_high(k)
            if k in EARLY_LOW:
                send_low(EARLY_LOW[k])
    for k in MID_LOW:
        send_low(k)

    gram = jnp.zeros((N_REP, LANES), jnp.float32)
    for k in range(CHUNKS):
        gram += gram_chunk(k)

    row = lax.broadcasted_iota(jnp.int32, (N_REP, LANES), 0)
    lane = lax.broadcasted_iota(jnp.int32, (N_REP, LANES), 1)
    folded = jnp.where(lane // N_REP == row % FOLD, gram, 0.0)
    folded = jnp.sum(folded.reshape(N_REP // FOLD, FOLD, LANES), axis=1)

    gram_own[0] = folded
    for peer in tp_peers:
        remote(
            gram_own.at[0], gram_tp.at[tp], gram_send.at[0], gram_recv.at[0], rep, peer
        ).start()
    for k in LATE_LOW:
        send_low(k)
    gram_tp[tp] = folded
    wait_bytes(gram_tp.at[pl.ds(0, N_TP - 1)], gram_recv.at[0])
    replica_sum = jnp.sum(gram_tp[...], axis=0)
    gram_own[1] = replica_sum
    for peer in rep_peers:
        remote(
            gram_own.at[1], gram_rep.at[rep], gram_send.at[1], gram_recv.at[1], peer, tp
        ).start()
    gram_rep[rep] = replica_sum

    for k in range(CHUNKS):
        wait_bytes(low_in.at[k, pl.ds(0, N_REP - 1)], low_recv.at[k])
        full[k] += low_in[k].astype(jnp.float32)
    for k in range(CHUNKS):
        wait_bytes(gathered.at[k, 0, pl.ds(0, NZ - 1)], ring_send.at[k])
        wait_bytes(gathered.at[k, 0], pair_send.at[k])
        wait_bytes(high_own.at[k, pl.ds(0, N_REP - 1)], high_send.at[k])
        wait_bytes(low_own.at[k, pl.ds(0, N_REP - 1)], low_send.at[k])
    wait_bytes(gram_tp.at[pl.ds(0, N_TP - 1)], gram_send.at[0])

    wait_bytes(gram_rep.at[pl.ds(0, N_REP - 1)], gram_recv.at[1])
    weights[...] = coefficients(jnp.sum(gram_rep[...], axis=0))
    for k in range(CHUNKS):
        combined = jnp.zeros((PACKED, LANES), jnp.float32)
        for r in range(N_REP):
            combined += weights[pl.ds(r, 1), :] * full[k, r]
        for p in range(PARTS):
            span = pl.ds(k * WIDTH + p * LANES, LANES)
            out_ref[:, span] = combined[p * ROWS:(p + 1) * ROWS]
    wait_bytes(gram_rep.at[pl.ds(0, N_REP - 1)], gram_send.at[1])


def body(activations, out_grad, weight, momentum):
    dma = pltpu.SemaphoreType.DMA
    combined = pl.pallas_call(
        kernel,
        out_shape=jax.ShapeDtypeStruct(momentum.shape, jnp.float32),
        in_specs=[pl.BlockSpec(memory_space=pltpu.HBM)] * 2,
        out_specs=pl.BlockSpec(memory_space=pltpu.VMEM),
        scratch_shapes=[
            pltpu.VMEM((TOKENS, FEATURES), jnp.bfloat16),
            pltpu.VMEM((FEATURES, TOKENS), jnp.bfloat16),
            pltpu.VMEM((CHUNKS, 2, NZ, BLOCK, WIDTH), jnp.bfloat16),
            pltpu.VMEM((CHUNKS, N_REP, PACKED, LANES), jnp.bfloat16),
            pltpu.VMEM((CHUNKS, N_REP, PACKED, LANES), jnp.bfloat16),
            pltpu.VMEM((CHUNKS, N_REP, PACKED, LANES), jnp.bfloat16),
            pltpu.VMEM((CHUNKS, N_REP, PACKED, LANES), jnp.bfloat16),
            pltpu.VMEM((CHUNKS, N_REP, PACKED, LANES), jnp.float32),
            pltpu.VMEM((2, ROWS, LANES), jnp.float32),
            pltpu.VMEM((N_REP, ROWS, LANES), jnp.float32),
            pltpu.VMEM((N_TP, ROWS, LANES), jnp.float32),
            pltpu.VMEM((N_REP, LANES), jnp.float32),
            dma,
            dma((CHUNKS,)),
            dma((CHUNKS,)),
            dma((CHUNKS, 2, NZ // 2)),
            dma((CHUNKS,)),
            dma((CHUNKS,)),
            dma((CHUNKS,)),
            dma((CHUNKS,)),
            dma((CHUNKS,)),
            dma((CHUNKS,)),
            dma((2,)),
            dma((2,)),
            pltpu.SemaphoreType.REGULAR((NY // 2,)),
        ],
        compiler_params=pltpu.CompilerParams(
            collective_id=0, has_side_effects=True, vmem_limit_bytes=56488960
        ),
    )(activations, out_grad)
    new_momentum = MOMENTUM_DECAY * momentum + combined
    new_weight = weight.astype(jnp.float32) - LEARNING_RATE * new_momentum
    return new_weight.astype(jnp.bfloat16), new_momentum


def solution(mesh):
    return jax.shard_map(
        body,
        mesh=mesh,
        in_specs=(
            P("rep", "tp"),
            P(("rep", "tp"), None),
            P(("tp", "rep"), None),
            P(("tp", "rep"), None),
        ),
        out_specs=(P(("tp", "rep"), None), P(("tp", "rep"), None)),
        check_vma=False,
    )
```

```python
import functools

import jax
import jax.numpy as jnp
from jax import lax
from jax.experimental import pallas as pl
from jax.experimental.pallas import tpu as pltpu
from jax.sharding import PartitionSpec as P

MOMENTUM_DECAY = 0.9
LEARNING_RATE = 0.02

NX, NY, NZ = 4, 8, 8
N_REP = NX * NY
N_TP = 2 * NZ
TOKENS = 2048
BLOCK = TOKENS // N_TP
FEATURES = 256
COLUMNS = 1024
ROWS = FEATURES // N_REP
CHUNKS = 4
WIDTH = COLUMNS // CHUNKS
HALF = BLOCK // 2
LANES = 128
FOLD = LANES // N_REP
PARTS = WIDTH // LANES
PACKED = ROWS * PARTS

MESH = pl.DeviceIdType.MESH


ORDER = (
    (0, 0), (1, 0), (2, 0), (0, 1), (3, 0), (1, 1), (0, 2), (2, 1), (1, 2), (0, 3),
    (3, 1), (2, 2), (1, 3), (0, 4), (3, 2), (2, 3), (1, 4), (3, 3), (2, 4), (3, 4),
)
TURN_AT = 3
PAIRED = {4: ((0, 8),)}
EARLY_LOW = {0: 0}
MID_LOW = (1, 2, 3)
LATE_LOW = ()
GREET = {4: 0, 7: 1, 10: 2, 12: 3}


def coefficients(gram):
    row = lax.broadcasted_iota(jnp.int32, (N_REP, LANES), 0)
    lane = lax.broadcasted_iota(jnp.int32, (N_REP, LANES), 1)
    column = lane % N_REP
    spread = jnp.broadcast_to(gram[:, None, :], (N_REP // FOLD, FOLD, LANES)).reshape(N_REP, LANES)
    kept = jnp.where(lane // N_REP == row % FOLD, spread, 0.0)
    kept = kept + pltpu.roll(kept, N_REP, 1)
    block = kept + pltpu.roll(kept, 2 * N_REP, 1)
    diagonal = row == column
    weights = jnp.ones((N_REP, LANES), jnp.float32)
    for level in range(N_REP.bit_length() - 1):
        apart = 1 << level
        own, other = jnp.where(diagonal, block, 0.0), jnp.where(row == (column ^ apart), block, 0.0)
        across = 1.0 - jnp.sum(other, axis=0, keepdims=True) / (
            2.0 * jnp.sum(own, axis=0, keepdims=True)
        )
        down = 1.0 - jnp.sum(other, axis=1, keepdims=True) / (
            2.0 * jnp.sum(own, axis=1, keepdims=True)
        )
        weights = weights * down
        if apart == N_REP // 2:
            break
        block = block * across * down
        upper = (column & apart) != 0
        block = block + jnp.where(
            upper, pltpu.roll(block, apart, 1), pltpu.roll(block, LANES - apart, 1)
        )
        upper = (row & apart) != 0
        block = block + jnp.where(
            upper, pltpu.roll(block, apart, 0), pltpu.roll(block, N_REP - apart, 0)
        )
    return weights


def kernel(
    a_ref, g_ref, out_ref,
    a_vmem, a_t, gathered, high_own, low_own, high_in, low_in, full,
    gram_own, gram_rep, gram_tp, weights,
    load_sem, own_sem, ring_send, ring_recv, pair_send, pair_recv, high_send, high_recv,
    low_send, low_recv, gram_send, gram_recv, greet_sem,
):
    rep = lax.axis_index("rep")
    tp = lax.axis_index("tp")
    y, x = rep // NX, lax.rem(rep, NX)
    z, core = tp // 2, lax.rem(tp, 2)
    sibling = z * 2 + (1 - core)
    ahead = lax.rem(z + 1, NZ) * 2 + core
    behind = lax.rem(z + NZ - 1, NZ) * 2 + core
    in_x = [lax.rem(x + d, NX) for d in range(NX)]
    far_x = sorted(range(NX), key=lambda d: -min(d, NX - d))
    far_y = sorted(range(NY), key=lambda d: -min(d, NY - d))
    far_z = sorted(range(NZ), key=lambda d: -min(d, NZ - d))
    in_y = [lax.rem(y + d, NY) * NX for d in range(NY)]
    rep_peers = [in_y[dy] + in_x[dx] for dy in far_y for dx in far_x if dy or dx]
    in_z = [lax.rem(z + d, NZ) * 2 for d in range(NZ)]
    tp_peers = [in_z[dz] + (core if same else 1 - core) for dz in far_z for same in (0, 1) if dz or not same]

    def remote(src, dst, send_sem, recv_sem, to_rep, to_tp):
        return pltpu.make_async_remote_copy(
            src_ref=src, dst_ref=dst, send_sem=send_sem, recv_sem=recv_sem,
            device_id=(to_rep, to_tp), device_id_type=MESH,
        )

    def wait_bytes(ref, sem):
        pltpu.make_async_copy(ref, ref, sem).wait()

    load = pltpu.make_async_copy(a_ref, a_vmem, load_sem)
    own_copies = [
        pltpu.make_async_copy(
            g_ref.at[:, pl.ds(k * WIDTH, WIDTH)], gathered.at[k, 0, 0], own_sem.at[k]
        )
        for k in range(CHUNKS)
    ]

    barrier = pltpu.get_barrier_semaphore()
    for peer in (sibling, ahead, behind):
        pl.semaphore_signal(barrier, inc=1, device_id=(rep, peer), device_id_type=MESH)
    for peer in [in_y[0] + in_x[d] for d in range(1, NX)] + [in_y[d] + x for d in (1, NY - 1)]:
        pl.semaphore_signal(barrier, inc=1, device_id=(peer, tp), device_id_type=MESH)

    def greet(turn):
        for d in (1, NY - 1):
            pl.semaphore_signal(
                greet_sem.at[turn], inc=1, device_id=(in_y[d] + x, tp), device_id_type=MESH
            )

    for copy in [load] + own_copies:
        copy.start()
    pl.semaphore_wait(barrier, 3 + NX - 1 + 2)
    greet(0)

    def ring_step(k, stage):
        middle = NZ // 2
        for way, to in ((0, ahead), (1, behind)):
            half = pl.ds(way * HALF, HALF)
            held, next_held = (stage, stage + 1) if way else (-stage % NZ, (-stage - 1) % NZ)
            if stage == 0:
                src = g_ref.at[:, pl.ds(k * WIDTH, WIDTH)]
            else:
                src = gathered.at[k, 0, held]
                came = gathered.at[k, 0, held, half] if stage == middle else src
                remote(
                    came, came, ring_send.at[k], ring_recv.at[k, way, stage - 1], rep, to
                ).wait_recv()
            if stage < middle:
                dst = gathered.at[k, 0, next_held]
                if stage == middle - 1:
                    src, dst = gathered.at[k, 0, held, half], gathered.at[k, 0, next_held, half]
                remote(
                    src, dst, ring_send.at[k], ring_recv.at[k, way, stage], rep, to
                ).start()
        for first, count in PAIRED.get(stage, ()):
            if first == 0:
                own_copies[k].wait()
            slots = pl.ds(first, count)
            remote(
                gathered.at[k, 0, slots], gathered.at[k, 1, slots],
                pair_send.at[k], pair_recv.at[k], rep, sibling,
            ).start()

    def send_rows(own, into, send_sem, recv_sem, k):
        def to(peer):
            remote(
                own.at[k, peer], into.at[k, rep], send_sem.at[k], recv_sem.at[k], peer, tp
            ).start()

        def to_row(dy):
            row = lax.rem(y + dy, NY) * NX
            for dx in far_x:
                to(row + in_x[dx])

        to_row(NY // 2)

        @pl.loop(1, NY // 2)
        def _(step):
            to_row(NY // 2 - step)
            to_row(NY // 2 + step)

        for dx in far_x:
            if dx:
                to(y * NX + in_x[dx])
        into[k, rep] = own[k, rep]

    def send_high(k):
        wait_bytes(gathered.at[k, 1], pair_recv.at[k])
        product = jnp.dot(
            a_t[...], gathered[k].reshape(TOKENS, WIDTH), preferred_element_type=jnp.float32
        )
        product = jnp.concatenate(
            [
                product[:, p * LANES:(p + 1) * LANES].reshape(N_REP, ROWS, LANES)
                for p in range(PARTS)
            ],
            axis=1,
        )
        high = product.astype(jnp.bfloat16)
        high_own[k] = high
        send_rows(high_own, high_in, high_send, high_recv, k)
        low_own[k] = (product - high.astype(jnp.float32)).astype(jnp.bfloat16)

    def send_low(k):
        send_rows(low_own, low_in, low_send, low_recv, k)

    def gram_chunk(k):
        wait_bytes(high_in.at[k, pl.ds(0, N_REP - 1)], high_recv.at[k])
        full[k] = high_in[k].astype(jnp.float32)
        total = jnp.zeros((N_REP, LANES), jnp.float32)
        for i in range(0, PACKED, 2):
            part = jnp.concatenate([full[k, :, i, :], full[k, :, i + 1, :]], axis=1)
            part = part.astype(jnp.bfloat16)
            total += lax.dot_general(
                part, jnp.concatenate([part] * FOLD, axis=0),
                (((1,), (1,)), ((), ())), preferred_element_type=jnp.float32,
            )
        return total

    for i, (k, stage) in enumerate(ORDER):
        if i == TURN_AT:
            load.wait()
            for j in range(N_TP):
                source = in_z[j % NZ] + (core if j < NZ else 1 - core)
                rows = pl.ds(pl.multiple_of(source * BLOCK, BLOCK), BLOCK)
                a_t[:, pl.ds(j * BLOCK, BLOCK)] = a_vmem[rows, :].T
        if i in GREET:
            turn = GREET[i]
            pl.semaphore_wait(greet_sem.at[turn], 2)
            if turn + 1 < NY // 2:
                greet(turn + 1)
        ring_step(k, stage)
        if stage == NZ // 2:
            send_high(k)
            if k in EARLY_LOW:
                send_low(EARLY_LOW[k])
    for k in MID_LOW:
        send_low(k)

    gram = jnp.zeros((N_REP, LANES), jnp.float32)
    for k in range(CHUNKS):
        gram += gram_chunk(k)

    row = lax.broadcasted_iota(jnp.int32, (N_REP, LANES), 0)
    lane = lax.broadcasted_iota(jnp.int32, (N_REP, LANES), 1)
    folded = jnp.where(lane // N_REP == row % FOLD, gram, 0.0)
    folded = jnp.sum(folded.reshape(N_REP // FOLD, FOLD, LANES), axis=1)

    gram_own[0] = folded
    for peer in tp_peers:
        remote(
            gram_own.at[0], gram_tp.at[tp], gram_send.at[0], gram_recv.at[0], rep, peer
        ).start()
    for k in LATE_LOW:
        send_low(k)
    gram_tp[tp] = folded
    wait_bytes(gram_tp.at[pl.ds(0, N_TP - 1)], gram_recv.at[0])
    replica_sum = jnp.sum(gram_tp[...], axis=0)
    gram_own[1] = replica_sum
    for peer in rep_peers:
        remote(
            gram_own.at[1], gram_rep.at[rep], gram_send.at[1], gram_recv.at[1], peer, tp
        ).start()
    gram_rep[rep] = replica_sum

    for k in range(CHUNKS):
        wait_bytes(low_in.at[k, pl.ds(0, N_REP - 1)], low_recv.at[k])
        full[k] += low_in[k].astype(jnp.float32)
    for k in range(CHUNKS):
        wait_bytes(gathered.at[k, 0, pl.ds(0, NZ - 1)], ring_send.at[k])
        wait_bytes(gathered.at[k, 0], pair_send.at[k])
        wait_bytes(high_own.at[k, pl.ds(0, N_REP - 1)], high_send.at[k])
        wait_bytes(low_own.at[k, pl.ds(0, N_REP - 1)], low_send.at[k])
    wait_bytes(gram_tp.at[pl.ds(0, N_TP - 1)], gram_send.at[0])

    wait_bytes(gram_rep.at[pl.ds(0, N_REP - 1)], gram_recv.at[1])
    weights[...] = coefficients(jnp.sum(gram_rep[...], axis=0))
    for k in range(CHUNKS):
        combined = jnp.zeros((PACKED, LANES), jnp.float32)
        for r in range(N_REP):
            combined += weights[pl.ds(r, 1), :] * full[k, r]
        for p in range(PARTS):
            span = pl.ds(k * WIDTH + p * LANES, LANES)
            out_ref[:, span] = combined[p * ROWS:(p + 1) * ROWS]
    wait_bytes(gram_rep.at[pl.ds(0, N_REP - 1)], gram_send.at[1])


def body(activations, out_grad, weight, momentum):
    dma = pltpu.SemaphoreType.DMA
    combined = pl.pallas_call(
        kernel,
        out_shape=jax.ShapeDtypeStruct(momentum.shape, jnp.float32),
        in_specs=[pl.BlockSpec(memory_space=pltpu.HBM)] * 2,
        out_specs=pl.BlockSpec(memory_space=pltpu.VMEM),
        scratch_shapes=[
            pltpu.VMEM((TOKENS, FEATURES), jnp.bfloat16),
            pltpu.VMEM((FEATURES, TOKENS), jnp.bfloat16),
            pltpu.VMEM((CHUNKS, 2, NZ, BLOCK, WIDTH), jnp.bfloat16),
            pltpu.VMEM((CHUNKS, N_REP, PACKED, LANES), jnp.bfloat16),
            pltpu.VMEM((CHUNKS, N_REP, PACKED, LANES), jnp.bfloat16),
            pltpu.VMEM((CHUNKS, N_REP, PACKED, LANES), jnp.bfloat16),
            pltpu.VMEM((CHUNKS, N_REP, PACKED, LANES), jnp.bfloat16),
            pltpu.VMEM((CHUNKS, N_REP, PACKED, LANES), jnp.float32),
            pltpu.VMEM((2, ROWS, LANES), jnp.float32),
            pltpu.VMEM((N_REP, ROWS, LANES), jnp.float32),
            pltpu.VMEM((N_TP, ROWS, LANES), jnp.float32),
            pltpu.VMEM((N_REP, LANES), jnp.float32),
            dma,
            dma((CHUNKS,)),
            dma((CHUNKS,)),
            dma((CHUNKS, 2, NZ // 2)),
            dma((CHUNKS,)),
            dma((CHUNKS,)),
            dma((CHUNKS,)),
            dma((CHUNKS,)),
            dma((CHUNKS,)),
            dma((CHUNKS,)),
            dma((2,)),
            dma((2,)),
            pltpu.SemaphoreType.REGULAR((NY // 2,)),
        ],
        compiler_params=pltpu.CompilerParams(
            collective_id=0, has_side_effects=True, vmem_limit_bytes=56488960
        ),
    )(activations, out_grad)
    new_momentum = MOMENTUM_DECAY * momentum + combined
    new_weight = weight.astype(jnp.float32) - LEARNING_RATE * new_momentum
    return new_weight.astype(jnp.bfloat16), new_momentum


def solution(mesh):
    return jax.shard_map(
        body,
        mesh=mesh,
        in_specs=(
            P("rep", "tp"),
            P(("rep", "tp"), None),
            P(("tp", "rep"), None),
            P(("tp", "rep"), None),
        ),
        out_specs=(P(("tp", "rep"), None), P(("tp", "rep"), None)),
        check_vma=False,
    )
```
